256 devices in a mesh: wide: 32 (over x_lo, z, core), narrow: 8 (over x_hi, y).
Axes of the slice: x: 4 (x_hi: 2, x_lo: 2; x = x_hi * 2 + x_lo), y: 4, z: 8, core: 2. Of those that a mesh axis runs over, the one named last changes fastest.
Arguments:
- points: bfloat16 [65536, 1024], P(('wide', 'narrow')), may hold values from -6 to 6
- seg_lengths: int32 [256, 32], P(('wide', 'narrow')), may hold values from 1 to 128, 256 in all within a row
- seg_owner: int32 [256, 32, 1], P(('wide', 'narrow')), may hold values from 0 to 7; in each aligned block of 32 rows (0 to 31, 32 to 63, ..., all dimensions but the last counted through in order) at most 8 rows name the same one
- seg_row: int32 [256, 32], P(('wide', 'narrow')), may hold values from 0 to 1535
- level_two: bfloat16 [131072, 1024], P('wide'), may hold values from -6 to 6
Outputs:
- means: float32 [12288, 1024], P('narrow', 'wide')
- scores: bfloat16 [12288, 131072], P('narrow', 'wide')
The draws below stay inside these ranges and needn't reach their ends.
Inputs may be any that keep to these rules, and one draw needn't show every extreme that they name: `seg_lengths`: each device's 32 lengths sum to 256; in every device's row one length equals 128. `seg_owner`: among the 32 runs of one device, at most 8 name the same owner; some device's runs name one owner exactly 8 times.
All inputs are finite; a program needn't handle non-finite values.
Results may differ from the reference program's by a relative error of at most 0.0049.
Values may be sent and summed in bfloat16 or wider, within the bound.
No kernel may reach another device: no remote copies, remote signals or barrier semaphores. Data moves between devices by JAX's collectives and lax.ppermute only.
A program may use at most 128 MiB of HBM per device.

```python
import math
import jax
import jax.numpy as jnp
import numpy as np
from jax import lax

D = 1024
PT_DEV = 256
SEGS = 32
MOST = 128
K1S = 1536
K2S = 4096
CAP = 8
POINTS = 65536
K2 = 131072
N_WIDE = 32
N_NARROW = 8


def place_ends(entries, own_key, low, high):
    extent = entries.shape
    place = [jax.random.randint(jax.random.fold_in(own_key, axis), (), 0, extent[axis]) for axis in range(len(extent))]
    entries = entries.at[tuple(place)].set(low)
    longest = extent.index(max(extent))
    place[longest] = (place[longest] + 1) % extent[longest]
    return entries.at[tuple(place)].set(high)


def shard_levels(key, dims, split, least, top_value):
    def one(dim, blocks):
        heights = jax.random.uniform(jax.random.fold_in(jax.random.fold_in(key, 6), dim), (blocks,), jnp.float32, least / len(split), top_value / len(split))
        return jnp.repeat(jnp.exp(heights), dims[dim] // blocks).reshape((-1,) + (1,) * (len(dims) - dim - 1))

    gain = one(*split[0])
    for cut in split[1:]:
        gain = gain * one(*cut)
    return gain


def profile(count, total, limit, lean):
    weights = [(1 << 20) // math.isqrt(standing ** lean) + 1 for standing in range(2, count + 1)]
    surplus, given = total - limit - (count - 1), [1] * (count - 1)
    while surplus > 0:
        movable = [i for i in range(count - 1) if given[i] < limit]
        mass, left = sum([weights[i] for i in movable]), surplus
        for i in movable:
            addition = min(limit - given[i], max(1, left * weights[i] // mass), surplus)
            given[i] = given[i] + addition
            surplus = surplus - addition
    return np.array([limit] + given)


def ragged(stream_key, number_of, total, reach, skew):
    if number_of == 2:
        one = jax.random.randint(stream_key, (), max(1, total - reach), min(reach, total - 1) + 1)
        return jnp.stack([one, total - one])
    tallies = jnp.asarray(profile(number_of, total, reach, skew), jnp.int32)
    twos = (number_of - 1) // 2
    donor, sink = tallies[1:1 + 2 * twos:2], tallies[2:2 + 2 * twos:2]
    room = jnp.minimum(donor - 1, reach - sink)
    shifted = jax.random.randint(jax.random.fold_in(stream_key, 1), (twos,), 0, 1 << 20) % (room + 1)
    tallies = tallies.at[1:1 + 2 * twos:2].set(donor - shifted).at[2:2 + 2 * twos:2].set(sink + shifted)
    return tallies[jax.random.permutation(jax.random.fold_in(stream_key, 2), number_of)]


def routed_block(own_key, own, number, rows, amount, top, most, skew):
    sequence = jax.random.permutation(own_key, amount)
    packed, ordinary = shares(amount, rows * top, most, skew, True), shares(amount, rows * top, most, skew, False)
    places = jnp.arange(amount)

    def named(sizes, rotation):
        used = int((sizes > 0).sum())
        fixed = max(1, used // 4)
        moved = fixed + (places - fixed + rotation * (used - fixed)) % max(1, amount - fixed)
        return jnp.zeros((amount,), jnp.int32).at[sequence[jnp.where(places < fixed, places, moved)]].set(jnp.asarray(sizes, jnp.int32))

    sizes = jnp.where(number % 4 == 0, named(packed, number // 4), named(ordinary, number - number // 4 - 1))
    mixed = jax.random.permutation(jax.random.fold_in(own, 3), amount)
    source_of, sink = mixed[0:amount // 2 * 2:2], mixed[1:amount // 2 * 2:2]
    room = jnp.minimum(sizes[source_of] - 1, most - sizes[sink]) // 2
    room = jnp.where((source_of == sequence[0]) | (sink == sequence[0]) | (sizes[sink] == 0), 0, jnp.maximum(room, 0))
    moved = jax.random.randint(jax.random.fold_in(own, 4), (amount // 2,), 0, 1 << 20) % (room + 1)
    sizes = sizes.at[source_of].add(-moved).at[sink].add(moved)
    members = jnp.searchsorted(jnp.cumsum(sizes), jnp.arange(rows * top), side="right").astype(jnp.int32)
    listing = members.reshape(top, rows).T
    listing = listing[jax.random.permutation(jax.random.fold_in(own, 1), rows)]
    rotation = jax.random.randint(jax.random.fold_in(own, 2), (rows, 1), 0, top)
    return jnp.take_along_axis(listing, (jnp.arange(top)[None, :] + rotation) % top, axis=1)


def shares(number_of, total, most, slope, full):
    weights = [(1 << 20) // math.isqrt(standing ** slope) + 1 for standing in range(1, number_of + 1)]
    largest = most if full else min(most, max(-(-total // number_of), total * weights[0] // sum(weights)))
    least = 1 if total - largest >= number_of - 1 else 0
    holding, spare = [largest] + [least] * (number_of - 1), total - largest - least * (number_of - 1)
    while spare > 0:
        candidates = [i for i in range(1, number_of) if holding[i] < largest] or [i for i in range(1, number_of) if holding[i] < most]
        mass, budget = sum([weights[i] for i in candidates]), spare
        for i in candidates:
            more = min(most - holding[i], max(1, budget * weights[i] // mass), spare)
            holding[i] = holding[i] + more
            spare = spare - more
    return np.array(holding)


def noise(key, extent, width, reach, split=(), kind=jnp.bfloat16):
    entries = width * jax.random.normal(key, extent, jnp.float32)
    if split:
        entries = entries * shard_levels(key, extent, split, -0.22, 0.18)
    return jnp.clip(entries, -reach, reach).astype(kind)


def setup_inputs(seed: int = 0) -> dict:
    arg_keys = jax.random.split(jax.random.key(seed), 6)
    points = noise(arg_keys[0], (POINTS, D), 1.0, 6.0, ((0, 256),))
    seg_lengths = jax.vmap(lambda own: ragged(own, SEGS, PT_DEV, MOST, 2))(jax.random.split(arg_keys[1], (N_WIDE * N_NARROW))).reshape((N_WIDE * N_NARROW, SEGS)).astype(jnp.int32)
    seg_owner_keys = jax.random.split(jax.random.fold_in(arg_keys[2], 1), (N_WIDE * N_NARROW) * SEGS // SEGS)
    seg_owner_turns = jax.random.permutation(jax.random.fold_in(arg_keys[2], 3), (N_WIDE * N_NARROW) * SEGS // SEGS)
    seg_owner = jax.vmap(lambda own, number: routed_block(jax.random.fold_in(arg_keys[2], 2), own, number, SEGS, N_NARROW, 1, CAP, 2))(seg_owner_keys, seg_owner_turns).reshape((N_WIDE * N_NARROW, SEGS, 1))
    seg_row = place_ends(jax.random.randint(arg_keys[3], (N_WIDE * N_NARROW, SEGS), 0, K1S), jax.random.fold_in(arg_keys[3], 1), 0, K1S - 1).astype(jnp.int32)
    level_two = noise(arg_keys[4], (K2, D), 1.0, 6.0, ((0, 32),))
    return dict(points=points, seg_lengths=seg_lengths, seg_owner=seg_owner, seg_row=seg_row, level_two=level_two)


def reference(points, seg_lengths, seg_owner, seg_row, level_two):
    blocks = points.reshape(N_WIDE * N_NARROW, PT_DEV, D)
    clusters = (seg_owner[:, :, 0] * K1S + seg_row).astype(jnp.int32)
    position = jnp.arange(PT_DEV, dtype=jnp.int32)

    def one_device(carry, item):
        block, lengths, ids = item
        ends = jnp.cumsum(lengths)
        starts = ends - lengths
        member = ((position[None, :] >= starts[:, None]) & (position[None, :] < ends[:, None])).astype(jnp.bfloat16)
        run_sums = jnp.dot(member, block, preferred_element_type=jnp.float32)
        total, tally = carry
        total = total.at[ids].add(run_sums)
        tally = tally.at[ids].add(lengths.astype(jnp.float32))
        return ((total, tally), None)
    start_state = (jnp.zeros((K1S * N_NARROW, D), jnp.float32), jnp.zeros((K1S * N_NARROW,), jnp.float32))
    (sums, counts), unused = lax.scan(one_device, start_state, (blocks, seg_lengths, clusters))
    means = sums / jnp.maximum(counts, 1.0)[:, None]
    unit = (sums / jnp.sqrt(lax.optimization_barrier(jnp.sum(sums * sums, axis=1)) + 1e-06)[:, None]).astype(jnp.bfloat16)
    level_blocks = level_two.reshape(N_WIDE, K2S, D)

    def score_block(piece):
        product = lax.dot_general(unit, piece, (((1,), (1,)), ((), ())), preferred_element_type=jnp.float32)
        return product.astype(jnp.bfloat16)
    scored = lax.map(score_block, level_blocks)
    scores = jnp.transpose(scored, (1, 0, 2)).reshape(K1S * N_NARROW, K2S * N_WIDE)
    return (means, scores)
```

```python
import jax
import jax.numpy as jnp
from jax import lax
from jax.experimental import pallas as pl
from jax.experimental.pallas import tpu as pltpu
from jax.sharding import PartitionSpec as P

K1S = 1536
K2S = 4096
D = 1024
HALF = 512
SEGS = 32
CAP = 8
NARROW = 8
SLOTS = 256
BLOCK = 272
LANES = 128
F32 = jnp.float32
BF16 = jnp.bfloat16

ALL = ("wide", "narrow")


def wide_of(x, z, c):
    return (x * 8 + z % 8) * 2 + c


WIDES = [(x, z, c) for x in range(2) for z in range(8) for c in range(2)]
PLANES = [
    [wide_of(x, z, c) * NARROW + n for x in range(2) for c in range(2) for n in range(NARROW)]
    for z in range(8)
]
CORE_SWAP = [(wide_of(x, z, c), wide_of(x, z, 1 - c)) for x, z, c in WIDES]


def z_shift(step):
    return [(wide_of(x, z, c), wide_of(x, z + step, c)) for x, z, c in WIDES]


def iota2(shape, axis):
    return lax.broadcasted_iota(jnp.int32, shape, axis)


def pack_kernel(points_ref, lengths_ref, owner_ref, rows_ref, out_ref):
    r, q = iota2((SEGS, SEGS), 0), iota2((SEGS, SEGS), 1)
    eye = (r == q).astype(F32)
    length_row = lengths_ref[...].astype(F32)
    id_row = rows_ref[...].astype(F32)
    length = jnp.sum(eye * length_row, axis=1, keepdims=True)
    ends = jnp.sum(jnp.where(q <= r, length_row, 0.0), axis=1, keepdims=True)
    ids = jnp.sum(eye * id_row, axis=1, keepdims=True)
    position = iota2((SEGS, 256), 1).astype(F32)
    member = ((position >= ends - length) & (position < ends)).astype(BF16)
    runs = jnp.dot(member, points_ref[...], preferred_element_type=F32).astype(BF16)

    owner = owner_ref[0].astype(F32)
    owner_row = jnp.sum(eye * owner, axis=0, keepdims=True)
    rank_row = jnp.sum(jnp.where((owner == owner_row) & (r < q), 1.0, 0.0), axis=0, keepdims=True)
    slot_row = owner_row * CAP + rank_row
    place = (iota2((NARROW * CAP, SEGS), 0).astype(F32) == slot_row).astype(BF16)
    slots = jnp.dot(place, runs, preferred_element_type=F32).astype(BF16)
    high = jnp.floor(ids * (1.0 / 16.0))
    low = ids - 16.0 * high
    lane = iota2((SEGS, LANES), 1)
    tags = jnp.where(lane == 0, high, jnp.where(lane == 1, low, jnp.where(lane == 2, length, 0.0)))
    tags = jnp.dot(place, tags.astype(BF16), preferred_element_type=F32).astype(BF16)
    per = NARROW * CAP
    for x in range(2):
        for c in range(2):
            at = pl.ds((x * 2 + c) * per, per)
            out_ref[at, :HALF] = slots[:, c * HALF : (c + 1) * HALF]
            out_ref[at, HALF:] = tags


def block_kernel(received_ref, out_ref):
    out_ref[:SLOTS, :] = received_ref[:, :HALF]
    tags = received_ref[:, HALF:].astype(F32)
    turned = jnp.concatenate([tags[:LANES].T[:16], tags[LANES:].T[:16]], axis=1)
    out_ref[SLOTS:, :SLOTS] = turned.astype(BF16)
    out_ref[SLOTS:, SLOTS:] = jnp.zeros((16, HALF - SLOTS), BF16)


CHUNK = 256


def place_kernel(*refs):
    blocks, sums_ref, counts_ref = refs[:-2], refs[-2], refs[-1]

    @pl.loop(0, K1S // CHUNK)
    def _(i):
        row = (iota2((CHUNK, SLOTS), 0) + i * CHUNK).astype(F32)
        total = jnp.zeros((CHUNK, HALF), F32)
        tally = jnp.zeros((CHUNK, 16), F32)
        for ref in blocks:
            tags = ref[SLOTS:, :SLOTS]
            ids = tags[0:1].astype(F32) * 16.0 + tags[1:2].astype(F32)
            hot = (row == ids).astype(BF16)
            total += jnp.dot(hot, ref[:SLOTS, :], preferred_element_type=F32)
            tally += lax.dot_general(hot, tags, (((1,), (1,)), ((), ())), preferred_element_type=F32)
        at = pl.ds(pl.multiple_of(i * CHUNK, CHUNK), CHUNK)
        sums_ref[at, :] = total.astype(BF16)
        counts_ref[at, :] = tally


TILE = 512


def score_kernel(own_ref, other_ref, counts_ref, two_ref, means_ref, scores_ref, sums, inverse):
    w = lax.axis_index("wide")
    core = w % 2

    @pl.when(pl.program_id(0) == 0)
    def _():
        sums[:, pl.ds(pl.multiple_of(core * HALF, HALF), HALF)] = own_ref[...]
        sums[:, pl.ds(pl.multiple_of((1 - core) * HALF, HALF), HALF)] = other_ref[...]

        @pl.loop(0, K1S // CHUNK)
        def _(i):
            at = pl.ds(pl.multiple_of(i * CHUNK, CHUNK), CHUNK)
            part = sums[at, :].astype(F32)
            square = jnp.sum(part * part, axis=1, keepdims=True)
            inverse[at, :] = jnp.broadcast_to(1.0 / jnp.sqrt(square + 1e-06), (CHUNK, LANES))
            lanes = pl.ds(pl.multiple_of(w // 4 * LANES, LANES), LANES)
            mine = pltpu.roll(sums[at, lanes].astype(F32), (4 - w % 4) % 4 * 32, 1)[:, :32]
            means_ref[at, :] = mine / jnp.maximum(counts_ref[at, 2:3], 1.0)

    @pl.loop(0, K1S // CHUNK)
    def _(i):
        at = pl.ds(pl.multiple_of(i * CHUNK, CHUNK), CHUNK)
        product = lax.dot_general(
            sums[at, :], two_ref[...], (((1,), (1,)), ((), ())), preferred_element_type=F32
        )
        scores_ref[at, :] = (product * inverse[at, 0:1]).astype(BF16)


def whole(shape):
    return pl.BlockSpec(shape, lambda *_: (0,) * len(shape))


def local(points, seg_lengths, seg_owner, seg_row, level_two):
    vmem = pl.BlockSpec(memory_space=pltpu.VMEM)
    send = pl.pallas_call(
        pack_kernel,
        out_shape=jax.ShapeDtypeStruct((SLOTS, HALF + LANES), BF16),
        in_specs=[vmem] * 4,
        out_specs=vmem,
        name="pack",
    )(points, seg_lengths, seg_owner, seg_row)
    received = lax.all_to_all(send, ALL, 0, 0, axis_index_groups=PLANES, tiled=True)
    block = pl.pallas_call(
        block_kernel,
        out_shape=jax.ShapeDtypeStruct((BLOCK, HALF), BF16),
        in_specs=[vmem],
        out_specs=vmem,
        name="block",
    )(received)

    up = down = block
    blocks = [block]
    for _ in range(3):
        up = lax.ppermute(up, "wide", z_shift(1))
        down = lax.ppermute(down, "wide", z_shift(-1))
        blocks += [up, down]
    last = lax.ppermute(up, "wide", z_shift(1))
    blocks.append(last)

    sums, counts = pl.pallas_call(
        place_kernel,
        out_shape=(jax.ShapeDtypeStruct((K1S, HALF), BF16), jax.ShapeDtypeStruct((K1S, 16), F32)),
        in_specs=[vmem] * len(blocks),
        out_specs=(vmem, vmem),
        compiler_params=pltpu.CompilerParams(vmem_limit_bytes=40 << 20),
        name="place",
    )(*blocks)
    other = lax.ppermute(sums, "wide", CORE_SWAP)

    means, scores = pl.pallas_call(
        score_kernel,
        grid=(K2S // TILE,),
        out_shape=(jax.ShapeDtypeStruct((K1S, 32), F32), jax.ShapeDtypeStruct((K1S, K2S), BF16)),
        in_specs=[
            whole((K1S, HALF)),
            whole((K1S, HALF)),
            whole((K1S, 16)),
            pl.BlockSpec((TILE, D), lambda j: (j, 0)),
        ],
        out_specs=(whole((K1S, 32)), pl.BlockSpec((K1S, TILE), lambda j: (0, j))),
        scratch_shapes=[pltpu.VMEM((K1S, D), BF16), pltpu.VMEM((K1S, LANES), F32)],
        compiler_params=pltpu.CompilerParams(vmem_limit_bytes=48 << 20),
        name="score",
    )(sums, other, counts, level_two)
    return means, scores


def solution(mesh):
    return jax.shard_map(
        local,
        mesh=mesh,
        in_specs=(
            P(ALL, None),
            P(ALL, None),
            P(ALL, None, None),
            P(ALL, None),
            P("wide", None),
        ),
        out_specs=(P("narrow", "wide"), P("narrow", "wide")),
        check_vma=False,
    )
```

```python
import jax
import jax.numpy as jnp
from jax import lax
from jax.experimental import pallas as pl
from jax.experimental.pallas import tpu as pltpu
from jax.sharding import PartitionSpec as P

K1S = 1536
K2S = 4096
D = 1024
HALF = 512
SEGS = 32
CAP = 8
NARROW = 8
SLOTS = 256
BLOCK = 272
LANES = 128
F32 = jnp.float32
BF16 = jnp.bfloat16

ALL = ("wide", "narrow")


def wide_of(x, z, c):
    return (x * 8 + z % 8) * 2 + c


WIDES = [(x, z, c) for x in range(2) for z in range(8) for c in range(2)]
PLANES = [
    [wide_of(x, z, c) * NARROW + n for x in range(2) for c in range(2) for n in range(NARROW)]
    for z in range(8)
]
CORE_SWAP = [(wide_of(x, z, c), wide_of(x, z, 1 - c)) for x, z, c in WIDES]
Z_FIRST = [(wide_of(x, z, c), wide_of(x, z + 1 - 2 * c, c)) for x, z, c in WIDES]
Z_SECOND = [(wide_of(x, z, c), wide_of(x, z - 1 + 2 * c, c)) for x, z, c in WIDES]


def iota2(shape, axis):
    return lax.broadcasted_iota(jnp.int32, shape, axis)


def pack_kernel(points_ref, lengths_ref, owner_ref, rows_ref, out_ref):
    r, q = iota2((SEGS, SEGS), 0), iota2((SEGS, SEGS), 1)
    eye = (r == q).astype(F32)
    length_row = lengths_ref[...].astype(F32)
    id_row = rows_ref[...].astype(F32)
    owner_row = owner_ref[...].astype(F32)
    length = jnp.sum(eye * length_row, axis=1, keepdims=True)
    ends = jnp.sum(jnp.where(q <= r, length_row, 0.0), axis=1, keepdims=True)
    ids = jnp.sum(eye * id_row, axis=1, keepdims=True)
    owner = jnp.sum(eye * owner_row, axis=1, keepdims=True)
    position = iota2((SEGS, 256), 1).astype(F32)
    member = ((position >= ends - length) & (position < ends)).astype(BF16)
    runs = jnp.dot(member, points_ref[...], preferred_element_type=F32).astype(BF16)

    rank_row = jnp.sum(jnp.where((owner == owner_row) & (r < q), 1.0, 0.0), axis=0, keepdims=True)
    slot_row = owner_row * CAP + rank_row
    place = (iota2((NARROW * CAP, SEGS), 0).astype(F32) == slot_row).astype(BF16)
    slots = jnp.dot(place, runs, preferred_element_type=F32).astype(BF16)
    high = jnp.floor(ids * (1.0 / 16.0))
    low = ids - 16.0 * high
    lane = iota2((SEGS, LANES), 1)
    tags = jnp.where(lane == 0, high, jnp.where(lane == 1, low, jnp.where(lane == 2, length, 0.0)))
    tags = jnp.dot(place, tags.astype(BF16), preferred_element_type=F32).astype(BF16)
    per = NARROW * CAP
    for x in range(2):
        for c in range(2):
            at = pl.ds((x * 2 + c) * per, per)
            out_ref[at, :HALF] = slots[:, c * HALF : (c + 1) * HALF]
            out_ref[at, HALF:] = tags


def block_kernel(received_ref, out_ref):
    out_ref[:SLOTS, :] = received_ref[:, :HALF]
    tags = received_ref[:, HALF:].astype(F32)
    turned = jnp.concatenate([tags[:LANES].T[:16], tags[LANES:].T[:16]], axis=1)
    out_ref[SLOTS:, :SLOTS] = turned.astype(BF16)
    out_ref[SLOTS:, SLOTS:] = jnp.zeros((16, HALF - SLOTS), BF16)


CHUNK = 256
NT = (((1,), (1,)), ((), ()))


def hot_rows(i, ref):
    tags = ref[SLOTS:, :SLOTS]
    ids = tags[0:1].astype(F32) * 16.0 + tags[1:2].astype(F32)
    row = (iota2((CHUNK, SLOTS), 0) + i * CHUNK).astype(F32)
    return (row == ids).astype(BF16), tags


def chunk(i):
    return pl.ds(pl.multiple_of(i * CHUNK, CHUNK), CHUNK)


def place(i, blocks, total, count):
    for ref in blocks:
        hot, tags = hot_rows(i, ref)
        total += jnp.dot(hot, ref[:SLOTS, :], preferred_element_type=F32)
        count += lax.dot_general(hot, tags, NT, preferred_element_type=F32)
    return total, count


def place_early_kernel(*refs):
    blocks, sums_ref, counts_ref, token_ref = refs[:-3], refs[-3], refs[-2], refs[-1]

    @pl.loop(0, K1S // CHUNK)
    def _(i):
        at = chunk(i)
        sums_ref[at, :], counts_ref[at, :] = place(
            i, blocks, jnp.zeros((CHUNK, HALF), F32), jnp.zeros((CHUNK, 16), F32)
        )

    token_ref[...] = jnp.zeros_like(token_ref)


def place_late_kernel(*refs):
    blocks, early_ref, tally_ref, sums_ref, counts_ref, rounded_ref = refs[:-5], *refs[-5:]

    @pl.loop(0, K1S // CHUNK)
    def _(i):
        at = chunk(i)
        total, count = place(i, blocks, early_ref[at, :], tally_ref[at, :])
        sums_ref[at, :] = total
        counts_ref[at, :] = count
        rounded_ref[at, :] = total.astype(BF16)


TILE = 512


def score_kernel(
    mine_ref, partner_ref, counts_ref, last_ref, last_partner_ref, two_ref,
    means_ref, scores_ref, sums, inverse,
):
    w = lax.axis_index("wide")
    core = w % 2

    @pl.when(pl.program_id(0) == 0)
    def _():
        @pl.loop(0, K1S // CHUNK)
        def _(i):
            at = chunk(i)
            hot, tags = hot_rows(i, last_ref)
            counts = counts_ref[at, :] + lax.dot_general(hot, tags, NT, preferred_element_type=F32)
            mine = mine_ref[at, :] + jnp.dot(hot, last_ref[:SLOTS, :], preferred_element_type=F32)
            other = partner_ref[at, :].astype(F32) + jnp.dot(
                hot, last_partner_ref[:SLOTS, :], preferred_element_type=F32
            )
            sums[at, pl.ds(pl.multiple_of(core * HALF, HALF), HALF)] = mine.astype(BF16)
            sums[at, pl.ds(pl.multiple_of((1 - core) * HALF, HALF), HALF)] = other.astype(BF16)
            square = jnp.sum(mine * mine + other * other, axis=1, keepdims=True)
            inverse[at, :] = jnp.broadcast_to(1.0 / jnp.sqrt(square + 1e-06), (CHUNK, LANES))
            lanes = pl.ds(pl.multiple_of(w // 4 * LANES, LANES), LANES)
            mean = pltpu.roll(sums[at, lanes].astype(F32), (4 - w % 4) % 4 * 32, 1)
            means_ref[:, at] = (mean / jnp.maximum(counts[:, 2:3], 1.0)).T[:32]

    product = lax.dot_general(sums[...], two_ref[...], NT, preferred_element_type=F32)
    scale = jnp.concatenate([inverse[...]] * (TILE // LANES), axis=1)
    scores_ref[...] = (product * scale).astype(BF16)


def whole(shape):
    return pl.BlockSpec(shape, lambda *_: (0,) * len(shape))


def cost(flops, moved):
    return pl.CostEstimate(flops=flops, bytes_accessed=moved, transcendentals=0)


def both(first, second):
    first = lax.ppermute(first, "wide", Z_FIRST)
    second = lax.ppermute(second, "wide", Z_SECOND)
    return lax.optimization_barrier((first, second))


def local(points, seg_lengths, seg_owner, seg_row, level_two):
    vmem = pl.BlockSpec(memory_space=pltpu.VMEM)
    send = pl.pallas_call(
        pack_kernel,
        out_shape=jax.ShapeDtypeStruct((SLOTS, HALF + LANES), BF16),
        in_specs=[vmem] * 4,
        out_specs=vmem,
        name="pack",
    )(points, seg_lengths, seg_owner.reshape(1, SEGS), seg_row)
    received = lax.all_to_all(send, ALL, 0, 0, axis_index_groups=PLANES, tiled=True)
    block = pl.pallas_call(
        block_kernel,
        out_shape=jax.ShapeDtypeStruct((BLOCK, HALF), BF16),
        in_specs=[vmem],
        out_specs=vmem,
        name="block",
    )(received)

    first = second = block
    blocks = [block]
    for _ in range(2):
        first, second = both(first, second)
        blocks += [first, second]

    totals = jax.ShapeDtypeStruct((K1S, HALF), F32)
    tallies = jax.ShapeDtypeStruct((K1S, 16), F32)
    small = pltpu.CompilerParams(vmem_limit_bytes=16 << 20)
    early, tally, token = pl.pallas_call(
        place_early_kernel,
        out_shape=(totals, tallies, jax.ShapeDtypeStruct((8, LANES), F32)),
        in_specs=[vmem] * 5,
        out_specs=(vmem, vmem, vmem),
        compiler_params=small,
        cost_estimate=cost(4 << 30, 4 << 20),
        name="place_early",
    )(*blocks)
    first, second = both(first, second)
    first, second, token = lax.optimization_barrier((first, second, token))
    last = lax.ppermute(first, "wide", Z_FIRST)
    mine, counts, rounded = pl.pallas_call(
        place_late_kernel,
        out_shape=(totals, tallies, jax.ShapeDtypeStruct((K1S, HALF), BF16)),
        in_specs=[vmem] * 4,
        out_specs=(vmem, vmem, vmem),
        compiler_params=small,
        cost_estimate=cost(4 << 30, 4 << 20),
        name="place_late",
    )(first, second, early, tally)
    partner = lax.ppermute(rounded, "wide", CORE_SWAP)
    last, partner = lax.optimization_barrier((last, partner))
    last_partner = lax.ppermute(last, "wide", CORE_SWAP)

    means, scores = pl.pallas_call(
        score_kernel,
        grid=(K2S // TILE,),
        out_shape=(
            jax.ShapeDtypeStruct((32, K1S), F32),
            jax.ShapeDtypeStruct((K1S, K2S), BF16),
        ),
        in_specs=[
            whole((K1S, HALF)),
            whole((K1S, HALF)),
            whole((K1S, 16)),
            whole((BLOCK, HALF)),
            whole((BLOCK, HALF)),
            pl.BlockSpec((TILE, D), lambda j: (j, 0)),
        ],
        out_specs=(whole((32, K1S)), pl.BlockSpec((K1S, TILE), lambda j: (0, j))),
        scratch_shapes=[pltpu.VMEM((K1S, D), BF16), pltpu.VMEM((K1S, LANES), F32)],
        compiler_params=pltpu.CompilerParams(vmem_limit_bytes=40 << 20),
        cost_estimate=cost(14 << 30, 24 << 20),
        name="score",
    )(mine, partner, counts, last, last_partner, level_two)
    return means.T, scores


def solution(mesh):
    return jax.shard_map(
        local,
        mesh=mesh,
        in_specs=(
            P(ALL, None),
            P(ALL, None),
            P(ALL, None, None),
            P(ALL, None),
            P("wide", None),
        ),
        out_specs=(P("narrow", "wide"), P("narrow", "wide")),
        check_vma=False,
    )
```

```python
import jax
import jax.numpy as jnp
from jax import lax
from jax.experimental import pallas as pl
from jax.experimental.pallas import tpu as pltpu
from jax.sharding import PartitionSpec as P

K1S = 1536
K2S = 4096
D = 1024
HALF = 512
SEGS = 32
CAP = 8
NARROW = 8
SLOTS = 256
BLOCK = 272
LANES = 128
F32 = jnp.float32
BF16 = jnp.bfloat16

ALL = ("wide", "narrow")


def wide_of(x, z, c):
    return (x * 8 + z % 8) * 2 + c


WIDES = [(x, z, c) for x in range(2) for z in range(8) for c in range(2)]
PLANES = [
    [wide_of(x, z, c) * NARROW + n for x in range(2) for c in range(2) for n in range(NARROW)]
    for z in range(8)
]
CORE_SWAP = [(wide_of(x, z, c), wide_of(x, z, 1 - c)) for x, z, c in WIDES]
Z_UP = [(wide_of(x, z, c), wide_of(x, z + 1, c)) for x, z, c in WIDES]
Z_DOWN = [(wide_of(x, z, c), wide_of(x, z - 1, c)) for x, z, c in WIDES]


def iota2(shape, axis):
    return lax.broadcasted_iota(jnp.int32, shape, axis)


def pack_kernel(points_ref, lengths_ref, owner_ref, rows_ref, out_ref):
    r, q = iota2((SEGS, SEGS), 0), iota2((SEGS, SEGS), 1)
    eye = (r == q).astype(F32)
    length_row = lengths_ref[...].astype(F32)
    id_row = rows_ref[...].astype(F32)
    owner_row = owner_ref[...].astype(F32)
    length = jnp.sum(eye * length_row, axis=1, keepdims=True)
    ends = jnp.sum(jnp.where(q <= r, length_row, 0.0), axis=1, keepdims=True)
    ids = jnp.sum(eye * id_row, axis=1, keepdims=True)
    owner = jnp.sum(eye * owner_row, axis=1, keepdims=True)
    position = iota2((SEGS, 256), 1).astype(F32)
    member = ((position >= ends - length) & (position < ends)).astype(BF16)
    runs = jnp.dot(member, points_ref[...], preferred_element_type=F32).astype(BF16)

    rank_row = jnp.sum(jnp.where((owner == owner_row) & (r < q), 1.0, 0.0), axis=0, keepdims=True)
    slot_row = owner_row * CAP + rank_row
    place = (iota2((NARROW * CAP, SEGS), 0).astype(F32) == slot_row).astype(BF16)
    slots = jnp.dot(place, runs, preferred_element_type=F32).astype(BF16)
    high = jnp.floor(ids * (1.0 / 16.0))
    low = ids - 16.0 * high
    lane = iota2((SEGS, LANES), 1)
    tags = jnp.where(lane == 0, high, jnp.where(lane == 1, low, jnp.where(lane == 2, length, 0.0)))
    tags = jnp.dot(place, tags.astype(BF16), preferred_element_type=F32).astype(BF16)
    per = NARROW * CAP
    for x in range(2):
        for c in range(2):
            at = pl.ds((x * 2 + c) * per, per)
            out_ref[at, :HALF] = slots[:, c * HALF : (c + 1) * HALF]
            out_ref[at, HALF:] = tags


def block_kernel(received_ref, out_ref):
    out_ref[:SLOTS, :] = received_ref[:, :HALF]
    tags = received_ref[:, HALF:].astype(F32)
    turned = jnp.concatenate([tags[:LANES].T[:16], tags[LANES:].T[:16]], axis=1)
    out_ref[SLOTS:, :SLOTS] = turned.astype(BF16)
    out_ref[SLOTS:, SLOTS:] = jnp.zeros((16, HALF - SLOTS), BF16)


CHUNK = 256
NT = (((1,), (1,)), ((), ()))


def hot_rows(start, rows, ref):
    tags = ref[SLOTS:, :SLOTS]
    ids = tags[0:1].astype(F32) * 16.0 + tags[1:2].astype(F32)
    row = (iota2((rows, SLOTS), 0) + start).astype(F32)
    return (row == ids).astype(BF16), tags


def chunk(i):
    return pl.ds(pl.multiple_of(i * CHUNK, CHUNK), CHUNK)


def place(i, blocks, total):
    for ref in blocks:
        total += jnp.dot(hot_rows(i * CHUNK, CHUNK, ref)[0], ref[:SLOTS, :], preferred_element_type=F32)
    return total


def place_early_kernel(*refs):
    blocks, sums_ref = refs[:-1], refs[-1]

    @pl.loop(0, K1S // CHUNK)
    def _(i):
        sums_ref[chunk(i), :] = place(i, blocks, jnp.zeros((CHUNK, HALF), F32))


def place_late_kernel(*refs):
    blocks, early_ref, sums_ref, rounded_ref = refs[:-3], *refs[-3:]

    @pl.loop(0, K1S // CHUNK)
    def _(i):
        total = place(i, blocks, early_ref[chunk(i), :])
        sums_ref[chunk(i), :] = total
        rounded_ref[chunk(i), :] = total.astype(BF16)


def count_kernel(*refs):
    blocks, counts_ref = refs[:-1], refs[-1]

    @pl.loop(0, K1S // CHUNK)
    def _(i):
        count = jnp.zeros((CHUNK, 16), F32)
        for ref in blocks:
            hot, tags = hot_rows(i * CHUNK, CHUNK, ref)
            count += lax.dot_general(hot, tags, NT, preferred_element_type=F32)
        counts_ref[chunk(i), :] = count


TILE = 512
PART = 768


def finish_kernel(sums_ref, tally_ref, last_ref, mine_ref, squares_ref, counts_ref):
    @pl.loop(0, K1S // CHUNK)
    def _(i):
        at = chunk(i)
        hot, tags = hot_rows(i * CHUNK, CHUNK, last_ref)
        counts_ref[at, :] = tally_ref[at, :] + lax.dot_general(hot, tags, NT, preferred_element_type=F32)
        mine = sums_ref[at, :] + jnp.dot(hot, last_ref[:SLOTS, :], preferred_element_type=F32)
        square = jnp.sum(mine * mine, axis=1, keepdims=True)
        mine_ref[at, :] = mine.astype(BF16)
        squares_ref[at, :] = jnp.broadcast_to(square, (CHUNK, LANES))


def score_kernel(
    mine_ref, squares_ref, counts_ref, partner_ref, last_ref, last_partner_ref, two_ref,
    means_ref, scores_ref, sums, inverse,
):
    w = lax.axis_index("wide")
    core = w % 2

    def score(at):
        product = lax.dot_general(sums[at, :], two_ref[...], NT, preferred_element_type=F32)
        scale = jnp.concatenate([inverse[at, :]] * (TILE // LANES), axis=1)
        scores_ref[at, :] = (product * scale).astype(BF16)

    @pl.when(pl.program_id(0) == 0)
    def _():
        for start in range(0, K1S, PART):
            at = pl.ds(start, PART)
            hot, _ = hot_rows(start, PART, last_ref)
            partner = partner_ref[at, :].astype(F32) + jnp.dot(
                hot, last_partner_ref[:SLOTS, :], preferred_element_type=F32
            )
            sums[at, pl.ds(pl.multiple_of(core * HALF, HALF), HALF)] = mine_ref[at, :]
            sums[at, pl.ds(pl.multiple_of((1 - core) * HALF, HALF), HALF)] = partner.astype(BF16)
            square = squares_ref[at, :] + jnp.sum(partner * partner, axis=1, keepdims=True)
            inverse[at, :] = 1.0 / jnp.sqrt(square + 1e-06)
            lanes = pl.ds(pl.multiple_of(w // 4 * LANES, LANES), LANES)
            mean = pltpu.roll(sums[at, lanes].astype(F32), (4 - w % 4) % 4 * 32, 1)
            means_ref[:, at] = (mean / jnp.maximum(counts_ref[at, 2:3], 1.0)).T[:32]
            score(at)

    @pl.when(pl.program_id(0) > 0)
    def _():
        score(pl.ds(0, K1S))


def whole(shape):
    return pl.BlockSpec(shape, lambda *_: (0,) * len(shape), pipeline_mode=pl.Buffered(1))


def cost(flops, moved):
    return pl.CostEstimate(flops=flops, bytes_accessed=moved, transcendentals=0)


def local(points, seg_lengths, seg_owner, seg_row, level_two):
    vmem = pl.BlockSpec(memory_space=pltpu.VMEM)
    send = pl.pallas_call(
        pack_kernel,
        out_shape=jax.ShapeDtypeStruct((SLOTS, HALF + LANES), BF16),
        in_specs=[vmem] * 4,
        out_specs=vmem,
        name="pack",
    )(points, seg_lengths, seg_owner.reshape(1, SEGS), seg_row)
    received = lax.all_to_all(send, ALL, 0, 0, axis_index_groups=PLANES, tiled=True)
    block = pl.pallas_call(
        block_kernel,
        out_shape=jax.ShapeDtypeStruct((BLOCK, HALF), BF16),
        in_specs=[vmem],
        out_specs=vmem,
        name="block",
    )(received)

    def placer(kernel, flops, out_shape, *operands):
        return pl.pallas_call(
            kernel,
            out_shape=out_shape,
            in_specs=[vmem] * len(operands),
            out_specs=jax.tree.map(lambda _: vmem, out_shape),
            compiler_params=pltpu.CompilerParams(vmem_limit_bytes=16 << 20),
            cost_estimate=cost(flops, 4 << 20),
            name=kernel.__name__[:-7],
        )(*operands)

    up = down = block
    blocks = [block]
    for _ in range(3):
        up, down = lax.ppermute(up, "wide", Z_UP), lax.ppermute(down, "wide", Z_DOWN)
        blocks += [up, down]
    last = lax.ppermute(down, "wide", Z_DOWN)

    totals, halves, tallies, squares_shape = [
        jax.ShapeDtypeStruct((K1S, n), t) for n, t in ((HALF, F32), (HALF, BF16), (16, F32), (LANES, F32))
    ]
    early = placer(place_early_kernel, 3 << 30, totals, *blocks[:5])
    sums, rounded = placer(place_late_kernel, 24 << 30, (totals, halves), up, down, early)
    partner = lax.ppermute(rounded, "wide", CORE_SWAP)
    tally = placer(count_kernel, 1 << 20, tallies, *blocks)
    last_partner = lax.ppermute(last, "wide", CORE_SWAP)
    mine, squares, counts = placer(
        finish_kernel, 24 << 30, (halves, squares_shape, tallies), sums, tally, last
    )

    means, scores = pl.pallas_call(
        score_kernel,
        grid=(K2S // TILE,),
        out_shape=(
            jax.ShapeDtypeStruct((32, K1S), F32),
            jax.ShapeDtypeStruct((K1S, K2S), BF16),
        ),
        in_specs=[
            *[vmem] * 6,
            pl.BlockSpec((TILE, D), lambda j: (j, 0)),
        ],
        out_specs=(whole((32, K1S)), pl.BlockSpec((K1S, TILE), lambda j: (0, j))),
        scratch_shapes=[pltpu.VMEM((K1S, D), BF16), pltpu.VMEM((K1S, LANES), F32)],
        compiler_params=pltpu.CompilerParams(vmem_limit_bytes=24 << 20),
        cost_estimate=cost(14 << 30, 24 << 20),
        name="score",
    )(mine, squares, counts, partner, last, last_partner, level_two)
    return means.T, scores


def solution(mesh):
    return jax.shard_map(
        local,
        mesh=mesh,
        in_specs=(
            P(ALL, None),
            P(ALL, None),
            P(ALL, None, None),
            P(ALL, None),
            P("wide", None),
        ),
        out_specs=(P("narrow", "wide"), P("narrow", "wide")),
        check_vma=False,
    )
```

```python
import jax
import jax.numpy as jnp
from jax import lax
from jax.experimental import pallas as pl
from jax.experimental.pallas import tpu as pltpu
from jax.sharding import PartitionSpec as P

K1S = 1536
K2S = 4096
D = 1024
HALF = 512
SEGS = 32
CAP = 8
NARROW = 8
SLOTS = 256
BLOCK = 272
LANES = 128
F32 = jnp.float32
BF16 = jnp.bfloat16

ALL = ("wide", "narrow")


def wide_of(x, z, c):
    return (x * 8 + z % 8) * 2 + c


WIDES = [(x, z, c) for x in range(2) for z in range(8) for c in range(2)]
PLANES = [
    [wide_of(x, z, c) * NARROW + n for x in range(2) for c in range(2) for n in range(NARROW)]
    for z in range(8)
]
CORE_SWAP = [(wide_of(x, z, c), wide_of(x, z, 1 - c)) for x, z, c in WIDES]
Z_UP = [(wide_of(x, z, c), wide_of(x, z + 1, c)) for x, z, c in WIDES]
Z_DOWN = [(wide_of(x, z, c), wide_of(x, z - 1, c)) for x, z, c in WIDES]


def iota2(shape, axis):
    return lax.broadcasted_iota(jnp.int32, shape, axis)


def pack_kernel(points_ref, lengths_ref, owner_ref, rows_ref, out_ref):
    r, q = iota2((SEGS, SEGS), 0), iota2((SEGS, SEGS), 1)
    eye = (r == q).astype(F32)
    length_row = lengths_ref[...].astype(F32)
    id_row = rows_ref[...].astype(F32)
    owner_row = owner_ref[...].astype(F32)
    length = jnp.sum(eye * length_row, axis=1, keepdims=True)
    ends = jnp.sum(jnp.where(q <= r, length_row, 0.0), axis=1, keepdims=True)
    ids = jnp.sum(eye * id_row, axis=1, keepdims=True)
    owner = jnp.sum(eye * owner_row, axis=1, keepdims=True)
    position = iota2((SEGS, 256), 1).astype(F32)
    member = ((position >= ends - length) & (position < ends)).astype(BF16)
    runs = jnp.dot(member, points_ref[...], preferred_element_type=F32).astype(BF16)

    rank_row = jnp.sum(jnp.where((owner == owner_row) & (r < q), 1.0, 0.0), axis=0, keepdims=True)
    slot_row = owner_row * CAP + rank_row
    place = (iota2((NARROW * CAP, SEGS), 0).astype(F32) == slot_row).astype(BF16)
    slots = jnp.dot(place, runs, preferred_element_type=F32).astype(BF16)
    high = jnp.floor(ids * (1.0 / 16.0))
    low = ids - 16.0 * high
    lane = iota2((SEGS, LANES), 1)
    tags = jnp.where(lane == 0, high, jnp.where(lane == 1, low, jnp.where(lane == 2, length, 0.0)))
    tags = jnp.dot(place, tags.astype(BF16), preferred_element_type=F32).astype(BF16)
    per = NARROW * CAP
    for x in range(2):
        for c in range(2):
            at = pl.ds((x * 2 + c) * per, per)
            out_ref[at, :HALF] = slots[:, c * HALF : (c + 1) * HALF]
            out_ref[at, HALF:] = tags


def block_kernel(received_ref, out_ref):
    out_ref[:SLOTS, :] = received_ref[:, :HALF]
    tags = received_ref[:, HALF:].astype(F32)
    turned = jnp.concatenate([tags[:LANES].T[:16], tags[LANES:].T[:16]], axis=1)
    out_ref[SLOTS:, :SLOTS] = turned.astype(BF16)
    out_ref[SLOTS:, SLOTS:] = jnp.zeros((16, HALF - SLOTS), BF16)


CHUNK = 256
NT = (((1,), (1,)), ((), ()))


def hot_rows(start, rows, ref):
    tags = ref[SLOTS:, :SLOTS]
    ids = tags[0:1].astype(F32) * 16.0 + tags[1:2].astype(F32)
    row = (iota2((rows, SLOTS), 0) + start).astype(F32)
    return (row == ids).astype(BF16), tags


def chunk(i):
    return pl.ds(pl.multiple_of(i * CHUNK, CHUNK), CHUNK)


def place(i, blocks, total):
    for ref in blocks:
        total += jnp.dot(hot_rows(i * CHUNK, CHUNK, ref)[0], ref[:SLOTS, :], preferred_element_type=F32)
    return total


def place_early_kernel(*refs):
    blocks, sums_ref = refs[:-1], refs[-1]

    @pl.loop(0, K1S // CHUNK)
    def _(i):
        sums_ref[chunk(i), :] = place(i, blocks, jnp.zeros((CHUNK, HALF), F32))


def place_late_kernel(*refs):
    blocks, early_ref, sums_ref, rounded_ref = refs[:-3], *refs[-3:]

    @pl.loop(0, K1S // CHUNK)
    def _(i):
        total = place(i, blocks, early_ref[chunk(i), :])
        sums_ref[chunk(i), :] = total
        rounded_ref[chunk(i), :] = total.astype(BF16)


def count_kernel(*refs):
    blocks, counts_ref = refs[:-1], refs[-1]

    @pl.loop(0, K1S // CHUNK)
    def _(i):
        count = jnp.zeros((CHUNK, 16), F32)
        for ref in blocks:
            hot, tags = hot_rows(i * CHUNK, CHUNK, ref)
            count += lax.dot_general(hot, tags, NT, preferred_element_type=F32)
        counts_ref[chunk(i), :] = count


TILE = 1024


def finish_kernel(sums_ref, tally_ref, last_ref, mine_ref, squares_ref, counts_ref):
    @pl.loop(0, K1S // CHUNK)
    def _(i):
        at = chunk(i)
        hot, tags = hot_rows(i * CHUNK, CHUNK, last_ref)
        counts_ref[at, :] = tally_ref[at, :] + lax.dot_general(hot, tags, NT, preferred_element_type=F32)
        mine = sums_ref[at, :] + jnp.dot(hot, last_ref[:SLOTS, :], preferred_element_type=F32)
        square = jnp.sum(mine * mine, axis=1, keepdims=True)
        mine_ref[at, :] = mine.astype(BF16)
        squares_ref[at, :] = jnp.broadcast_to(square, (CHUNK, LANES))


def score_kernel(
    mine_ref, squares_ref, counts_ref, partner_ref, last_ref, last_partner_ref, two_ref,
    means_ref, scores_ref, sums, inverse,
):
    w = lax.axis_index("wide")
    core = w % 2

    def score():
        product = lax.dot_general(sums[...], two_ref[...], NT, preferred_element_type=F32)
        scale = jnp.concatenate([inverse[...]] * (TILE // LANES), axis=1)
        scores_ref[...] = (product * scale).astype(BF16)

    @pl.when(pl.program_id(0) == 0)
    def _():
        hot, _ = hot_rows(0, K1S, last_ref)
        partner = partner_ref[...].astype(F32) + jnp.dot(
            hot, last_partner_ref[:SLOTS, :], preferred_element_type=F32
        )
        sums[:, pl.ds(pl.multiple_of(core * HALF, HALF), HALF)] = mine_ref[...]
        sums[:, pl.ds(pl.multiple_of((1 - core) * HALF, HALF), HALF)] = partner.astype(BF16)
        square = squares_ref[...] + jnp.sum(partner * partner, axis=1, keepdims=True)
        inverse[...] = 1.0 / jnp.sqrt(square + 1e-06)
        lanes = pl.ds(pl.multiple_of(w // 4 * LANES, LANES), LANES)
        mean = pltpu.roll(sums[:, lanes].astype(F32), (4 - w % 4) % 4 * 32, 1)
        means_ref[...] = (mean / jnp.maximum(counts_ref[:, 2:3], 1.0)).T[:32]
        score()

    @pl.when(pl.program_id(0) > 0)
    def _():
        score()


def whole(shape):
    return pl.BlockSpec(shape, lambda *_: (0,) * len(shape), pipeline_mode=pl.Buffered(1))


def cost(flops, moved):
    return pl.CostEstimate(flops=flops, bytes_accessed=moved, transcendentals=0)


def local(points, seg_lengths, seg_owner, seg_row, level_two):
    vmem = pl.BlockSpec(memory_space=pltpu.VMEM)
    send = pl.pallas_call(
        pack_kernel,
        out_shape=pltpu.VMEM((SLOTS, HALF + LANES), BF16),
        in_specs=[vmem] * 4,
        out_specs=vmem,
        name="pack",
    )(points, seg_lengths, seg_owner.reshape(1, SEGS), seg_row)
    received = lax.all_to_all(send, ALL, 0, 0, axis_index_groups=PLANES, tiled=True)
    block = pl.pallas_call(
        block_kernel,
        out_shape=pltpu.VMEM((BLOCK, HALF), BF16),
        in_specs=[vmem],
        out_specs=vmem,
        name="block",
    )(received)

    def placer(kernel, flops, out_shape, *operands):
        return pl.pallas_call(
            kernel,
            out_shape=out_shape,
            in_specs=[vmem] * len(operands),
            out_specs=jax.tree.map(lambda _: vmem, out_shape),
            compiler_params=pltpu.CompilerParams(vmem_limit_bytes=16 << 20),
            cost_estimate=cost(flops, 4 << 20),
            name=kernel.__name__[:-7],
        )(*operands)

    up = down = block
    blocks = [block]
    for _ in range(3):
        up, down = lax.ppermute(up, "wide", Z_UP), lax.ppermute(down, "wide", Z_DOWN)
        blocks += [up, down]
    last = lax.ppermute(down, "wide", Z_DOWN)

    totals, halves, tallies, squares_shape = [
        jax.ShapeDtypeStruct((K1S, n), t) for n, t in ((HALF, F32), (HALF, BF16), (16, F32), (LANES, F32))
    ]
    early = placer(place_early_kernel, 3 << 30, totals, *blocks[:5])
    sums, rounded = placer(place_late_kernel, 24 << 30, (totals, halves), up, down, early)
    partner = lax.ppermute(rounded, "wide", CORE_SWAP)
    tally = placer(count_kernel, 1 << 20, tallies, *blocks)
    last_partner = lax.ppermute(last, "wide", CORE_SWAP)
    mine, squares, counts = placer(
        finish_kernel, 24 << 30, (halves, squares_shape, tallies), sums, tally, last
    )

    means, scores = pl.pallas_call(
        score_kernel,
        grid=(K2S // TILE,),
        out_shape=(
            jax.ShapeDtypeStruct((32, K1S), F32),
            jax.ShapeDtypeStruct((K1S, K2S), BF16),
        ),
        in_specs=[
            *[vmem] * 6,
            pl.BlockSpec((TILE, D), lambda j: (j, 0)),
        ],
        out_specs=(whole((32, K1S)), pl.BlockSpec((K1S, TILE), lambda j: (0, j))),
        scratch_shapes=[pltpu.VMEM((K1S, D), BF16), pltpu.VMEM((K1S, LANES), F32)],
        compiler_params=pltpu.CompilerParams(vmem_limit_bytes=32 << 20),
        cost_estimate=cost(14 << 30, 24 << 20),
        name="score",
    )(mine, squares, counts, partner, last, last_partner, level_two)
    return means.T, scores


def solution(mesh):
    return jax.shard_map(
        local,
        mesh=mesh,
        in_specs=(
            P(ALL, None),
            P(ALL, None),
            P(ALL, None, None),
            P(ALL, None),
            P("wide", None),
        ),
        out_specs=(P("narrow", "wide"), P("narrow", "wide")),
        check_vma=False,
    )
```

```python
import jax
import jax.numpy as jnp
from jax import lax
from jax.experimental import pallas as pl
from jax.experimental.pallas import tpu as pltpu
from jax.sharding import PartitionSpec as P

K1S = 1536
K2S = 4096
D = 1024
HALF = 512
SEGS = 32
CAP = 8
NARROW = 8
SLOTS = 256
BLOCK = 264
LANES = 128
F32 = jnp.float32
BF16 = jnp.bfloat16

ALL = ("wide", "narrow")


def wide_of(x, z, c):
    return (x * 8 + z % 8) * 2 + c


WIDES = [(x, z, c) for x in range(2) for z in range(8) for c in range(2)]
PLANES = [
    [wide_of(x, z, c) * NARROW + n for x in range(2) for c in range(2) for n in range(NARROW)]
    for z in range(8)
]
CORE_SWAP = [(wide_of(x, z, c), wide_of(x, z, 1 - c)) for x, z, c in WIDES]
Z_UP = [(wide_of(x, z, c), wide_of(x, z + 1, c)) for x, z, c in WIDES]
Z_DOWN = [(wide_of(x, z, c), wide_of(x, z - 1, c)) for x, z, c in WIDES]


def iota2(shape, axis):
    return lax.broadcasted_iota(jnp.int32, shape, axis)


def pack_kernel(points_ref, lengths_ref, owner_ref, rows_ref, out_ref):
    r, q = iota2((SEGS, SEGS), 0), iota2((SEGS, SEGS), 1)
    eye = (r == q).astype(F32)
    length_row = lengths_ref[...].astype(F32)
    id_row = rows_ref[...].astype(F32)
    owner_row = owner_ref[...].astype(F32)
    length = jnp.sum(eye * length_row, axis=1, keepdims=True)
    ends = jnp.sum(jnp.where(q <= r, length_row, 0.0), axis=1, keepdims=True)
    ids = jnp.sum(eye * id_row, axis=1, keepdims=True)
    owner = jnp.sum(eye * owner_row, axis=1, keepdims=True)
    position = iota2((SEGS, 256), 1).astype(F32)
    member = ((position >= ends - length) & (position < ends)).astype(BF16)
    runs = jnp.dot(member, points_ref[...], preferred_element_type=F32).astype(BF16)

    rank_row = jnp.sum(jnp.where((owner == owner_row) & (r < q), 1.0, 0.0), axis=0, keepdims=True)
    slot_row = owner_row * CAP + rank_row
    place = (iota2((NARROW * CAP, SEGS), 0).astype(F32) == slot_row).astype(BF16)
    slots = jnp.dot(place, runs, preferred_element_type=F32).astype(BF16)
    high = jnp.floor(ids * (1.0 / 16.0))
    low = ids - 16.0 * high
    lane = iota2((SEGS, LANES), 1)
    tags = jnp.where(lane == 0, high, jnp.where(lane == 1, low, jnp.where(lane == 2, length, 0.0)))
    tags = jnp.dot(place, tags.astype(BF16), preferred_element_type=F32).astype(BF16)
    per = NARROW * CAP
    for x in range(2):
        for c in range(2):
            at = pl.ds((x * 2 + c) * per, per)
            out_ref[at, :HALF] = slots[:, c * HALF : (c + 1) * HALF]
            out_ref[at, HALF:] = tags


def block_kernel(received_ref, out_ref):
    out_ref[:SLOTS, :] = received_ref[:, :HALF]
    tags = received_ref[:, HALF:].astype(F32)
    turned = jnp.concatenate([tags[:LANES].T[:8], tags[LANES:].T[:8]], axis=1)
    out_ref[SLOTS:, :SLOTS] = turned.astype(BF16)
    out_ref[SLOTS:, SLOTS:] = jnp.zeros((8, HALF - SLOTS), BF16)


CHUNK = 768
NT = (((1,), (1,)), ((), ()))


def hot_rows(start, rows, ref):
    tags = ref[SLOTS:, :SLOTS]
    ids = tags[0:1].astype(F32) * 16.0 + tags[1:2].astype(F32)
    row = (iota2((rows, SLOTS), 0) + start).astype(F32)
    return (row == ids).astype(BF16), tags


def chunk(i):
    return pl.ds(pl.multiple_of(i * CHUNK, CHUNK), CHUNK)


def place(i, blocks, total):
    for ref in blocks:
        total += jnp.dot(hot_rows(i * CHUNK, CHUNK, ref)[0], ref[:SLOTS, :], preferred_element_type=F32)
    return total


def fetch_kernel(two_ref, out_ref, token_ref, arrived):
    copy = pltpu.make_async_copy(two_ref, out_ref, arrived)
    copy.start()
    token_ref[...] = jnp.zeros_like(token_ref)
    copy.wait()


def place_early_kernel(*refs):
    blocks, sums_ref = refs[:-2], refs[-1]

    @pl.loop(0, K1S // CHUNK)
    def _(i):
        sums_ref[chunk(i), :] = place(i, blocks, jnp.zeros((CHUNK, HALF), F32))


def place_late_kernel(*refs):
    blocks, early_ref, sums_ref, rounded_ref = refs[:-3], *refs[-3:]

    @pl.loop(0, K1S // CHUNK)
    def _(i):
        total = place(i, blocks, early_ref[chunk(i), :])
        sums_ref[chunk(i), :] = total
        rounded_ref[chunk(i), :] = total.astype(BF16)


def count_kernel(*refs):
    blocks, counts_ref = refs[:-1], refs[-1]

    @pl.loop(0, K1S // CHUNK)
    def _(i):
        count = jnp.zeros((CHUNK, 8), F32)
        for ref in blocks:
            hot, tags = hot_rows(i * CHUNK, CHUNK, ref)
            count += lax.dot_general(hot, tags, NT, preferred_element_type=F32)
        counts_ref[chunk(i), :] = count


TILE = 1024


def finish_kernel(sums_ref, tally_ref, last_ref, mine_ref, squares_ref, counts_ref):
    @pl.loop(0, K1S // CHUNK)
    def _(i):
        at = chunk(i)
        hot, tags = hot_rows(i * CHUNK, CHUNK, last_ref)
        counts_ref[at, :] = tally_ref[at, :] + lax.dot_general(hot, tags, NT, preferred_element_type=F32)
        mine = sums_ref[at, :] + jnp.dot(hot, last_ref[:SLOTS, :], preferred_element_type=F32)
        square = jnp.sum(mine * mine, axis=1, keepdims=True)
        mine_ref[at, :] = mine.astype(BF16)
        squares_ref[at, :] = jnp.broadcast_to(square, (CHUNK, LANES))


def score_kernel(
    mine_ref, squares_ref, counts_ref, partner_ref, last_ref, last_partner_ref, two_ref,
    means_ref, scores_ref, sums, inverse,
):
    w = lax.axis_index("wide")
    core = w % 2

    def score():
        product = lax.dot_general(sums[...], two_ref[...], NT, preferred_element_type=F32)
        scale = jnp.concatenate([inverse[...]] * (TILE // LANES), axis=1)
        scores_ref[...] = (product * scale).astype(BF16)

    @pl.when(pl.program_id(0) == 0)
    def _():
        hot, _ = hot_rows(0, K1S, last_ref)
        partner = partner_ref[...].astype(F32) + jnp.dot(
            hot, last_partner_ref[:SLOTS, :], preferred_element_type=F32
        )
        sums[:, pl.ds(pl.multiple_of(core * HALF, HALF), HALF)] = mine_ref[...]
        sums[:, pl.ds(pl.multiple_of((1 - core) * HALF, HALF), HALF)] = partner.astype(BF16)
        square = squares_ref[...] + jnp.sum(partner * partner, axis=1, keepdims=True)
        inverse[...] = 1.0 / jnp.sqrt(square + 1e-06)
        lanes = pl.ds(pl.multiple_of(w // 4 * LANES, LANES), LANES)
        mean = pltpu.roll(sums[:, lanes].astype(F32), (4 - w % 4) % 4 * 32, 1)
        means_ref[...] = (mean / jnp.maximum(counts_ref[:, 2:3], 1.0)).T[:32]
        score()

    @pl.when(pl.program_id(0) > 0)
    def _():
        score()


def whole(shape):
    return pl.BlockSpec(shape, lambda *_: (0,) * len(shape), pipeline_mode=pl.Buffered(1))


def cost(flops, moved):
    return pl.CostEstimate(flops=flops, bytes_accessed=moved, transcendentals=0)


def local(points, seg_lengths, seg_owner, seg_row, level_two):
    vmem = pl.BlockSpec(memory_space=pltpu.VMEM)
    send = pl.pallas_call(
        pack_kernel,
        out_shape=pltpu.VMEM((SLOTS, HALF + LANES), BF16),
        in_specs=[vmem] * 4,
        out_specs=vmem,
        name="pack",
    )(points, seg_lengths, seg_owner.reshape(1, SEGS), seg_row)
    received = lax.all_to_all(send, ALL, 0, 0, axis_index_groups=PLANES, tiled=True)
    block = pl.pallas_call(
        block_kernel,
        out_shape=pltpu.VMEM((BLOCK, HALF), BF16),
        in_specs=[vmem],
        out_specs=vmem,
        name="block",
    )(received)

    def placer(kernel, flops, out_shape, *operands):
        return pl.pallas_call(
            kernel,
            out_shape=out_shape,
            in_specs=[vmem] * len(operands),
            out_specs=jax.tree.map(lambda _: vmem, out_shape),
            compiler_params=pltpu.CompilerParams(vmem_limit_bytes=16 << 20),
            cost_estimate=cost(flops, 4 << 20),
            name=kernel.__name__[:-7],
        )(*operands)

    up = down = block
    blocks = [block]
    for _ in range(3):
        up, down = lax.ppermute(up, "wide", Z_UP), lax.ppermute(down, "wide", Z_DOWN)
        blocks += [up, down]
    last = lax.ppermute(down, "wide", Z_DOWN)

    totals, halves, tallies, squares_shape = [
        jax.ShapeDtypeStruct((K1S, n), t) for n, t in ((HALF, F32), (HALF, BF16), (8, F32), (LANES, F32))
    ]
    level_two, token = pl.pallas_call(
        fetch_kernel,
        out_shape=(pltpu.VMEM((K2S, D), BF16), jax.ShapeDtypeStruct((8, LANES), F32)),
        in_specs=[pl.BlockSpec(memory_space=pl.ANY)],
        out_specs=(vmem, vmem),
        scratch_shapes=[pltpu.SemaphoreType.DMA],
        compiler_params=pltpu.CompilerParams(vmem_limit_bytes=12 << 20),
        cost_estimate=cost(3 << 30, 8 << 20),
        name="fetch",
    )(level_two)
    early = placer(place_early_kernel, 24 << 30, totals, *blocks[:5], token)
    sums, rounded = placer(place_late_kernel, 24 << 30, (totals, halves), up, down, early)
    partner = lax.ppermute(rounded, "wide", CORE_SWAP)
    tally = placer(count_kernel, 1 << 20, tallies, *blocks)
    last_partner = lax.ppermute(last, "wide", CORE_SWAP)
    mine, squares, counts = placer(
        finish_kernel, 24 << 30, (halves, squares_shape, tallies), sums, tally, last
    )

    means, scores = pl.pallas_call(
        score_kernel,
        grid=(K2S // TILE,),
        out_shape=(
            jax.ShapeDtypeStruct((32, K1S), F32),
            jax.ShapeDtypeStruct((K1S, K2S), BF16),
        ),
        in_specs=[
            *[vmem] * 6,
            pl.BlockSpec((TILE, D), lambda j: (j, 0)),
        ],
        out_specs=(whole((32, K1S)), pl.BlockSpec((K1S, TILE), lambda j: (0, j))),
        scratch_shapes=[pltpu.VMEM((K1S, D), BF16), pltpu.VMEM((K1S, LANES), F32)],
        compiler_params=pltpu.CompilerParams(vmem_limit_bytes=32 << 20),
        cost_estimate=cost(14 << 30, 24 << 20),
        name="score",
    )(mine, squares, counts, partner, last, last_partner, level_two)
    return means.T, scores


def solution(mesh):
    return jax.shard_map(
        local,
        mesh=mesh,
        in_specs=(
            P(ALL, None),
            P(ALL, None),
            P(ALL, None, None),
            P(ALL, None),
            P("wide", None),
        ),
        out_specs=(P("narrow", "wide"), P("narrow", "wide")),
        check_vma=False,
    )
```

```python
import jax
import jax.numpy as jnp
from jax import lax
from jax.experimental import pallas as pl
from jax.experimental.pallas import tpu as pltpu
from jax.sharding import PartitionSpec as P

K1S = 1536
K2S = 4096
D = 1024
HALF = 512
SEGS = 32
CAP = 8
NARROW = 8
SLOTS = 256
BLOCK = 264
LANES = 128
F32 = jnp.float32
BF16 = jnp.bfloat16

ALL = ("wide", "narrow")


def wide_of(x, z, c):
    return (x * 8 + z % 8) * 2 + c


WIDES = [(x, z, c) for x in range(2) for z in range(8) for c in range(2)]
PLANES = [
    [wide_of(x, z, c) * NARROW + n for x in range(2) for c in range(2) for n in range(NARROW)]
    for z in range(8)
]
CORE_SWAP = [(wide_of(x, z, c), wide_of(x, z, 1 - c)) for x, z, c in WIDES]
Z_UP = [(wide_of(x, z, c), wide_of(x, z + 1, c)) for x, z, c in WIDES]
Z_DOWN = [(wide_of(x, z, c), wide_of(x, z - 1, c)) for x, z, c in WIDES]


def iota2(shape, axis):
    return lax.broadcasted_iota(jnp.int32, shape, axis)


def pack_kernel(points_ref, lengths_ref, owner_ref, rows_ref, out_ref):
    r, q = iota2((SEGS, SEGS), 0), iota2((SEGS, SEGS), 1)
    eye = (r == q).astype(F32)
    length_row = lengths_ref[...].astype(F32)
    id_row = rows_ref[...].astype(F32)
    owner_row = owner_ref[...].astype(F32)
    length = jnp.sum(eye * length_row, axis=1, keepdims=True)
    ends = jnp.sum(jnp.where(q <= r, length_row, 0.0), axis=1, keepdims=True)
    ids = jnp.sum(eye * id_row, axis=1, keepdims=True)
    owner = jnp.sum(eye * owner_row, axis=1, keepdims=True)
    position = iota2((SEGS, 256), 1).astype(F32)
    member = ((position >= ends - length) & (position < ends)).astype(BF16)
    runs = jnp.dot(member, points_ref[...], preferred_element_type=F32).astype(BF16)

    rank_row = jnp.sum(jnp.where((owner == owner_row) & (r < q), 1.0, 0.0), axis=0, keepdims=True)
    slot_row = owner_row * CAP + rank_row
    place = (iota2((NARROW * CAP, SEGS), 0).astype(F32) == slot_row).astype(BF16)
    slots = jnp.dot(place, runs, preferred_element_type=F32).astype(BF16)
    high = jnp.floor(ids * (1.0 / 16.0))
    low = ids - 16.0 * high
    lane = iota2((SEGS, LANES), 1)
    tags = jnp.where(lane == 0, high, jnp.where(lane == 1, low, jnp.where(lane == 2, length, 0.0)))
    tags = jnp.dot(place, tags.astype(BF16), preferred_element_type=F32).astype(BF16)
    per = NARROW * CAP
    for x in range(2):
        for c in range(2):
            at = pl.ds((x * 2 + c) * per, per)
            out_ref[at, :HALF] = slots[:, c * HALF : (c + 1) * HALF]
            out_ref[at, HALF:] = tags


def block_kernel(received_ref, out_ref):
    out_ref[:SLOTS, :] = received_ref[:, :HALF]
    tags = received_ref[:, HALF:].astype(F32)
    turned = jnp.concatenate([tags[:LANES].T[:8], tags[LANES:].T[:8]], axis=1)
    out_ref[SLOTS:, :SLOTS] = turned.astype(BF16)
    out_ref[SLOTS:, SLOTS:] = jnp.zeros((8, HALF - SLOTS), BF16)


CHUNK = 768
NT = (((1,), (1,)), ((), ()))


def hot_rows(start, rows, ref):
    tags = ref[SLOTS:, :SLOTS]
    ids = tags[0:1].astype(F32) * 16.0 + tags[1:2].astype(F32)
    row = (iota2((rows, SLOTS), 0) + start).astype(F32)
    return (row == ids).astype(BF16), tags


def chunk(i):
    return pl.ds(pl.multiple_of(i * CHUNK, CHUNK), CHUNK)


def place(i, blocks, total):
    for ref in blocks:
        total += jnp.dot(hot_rows(i * CHUNK, CHUNK, ref)[0], ref[:SLOTS, :], preferred_element_type=F32)
    return total


def fetch_kernel(two_ref, out_ref, token_ref, arrived):
    copy = pltpu.make_async_copy(two_ref, out_ref, arrived)
    copy.start()
    token_ref[...] = jnp.zeros_like(token_ref)
    copy.wait()


def place_early_kernel(*refs):
    blocks, sums_ref = refs[:-2], refs[-1]

    @pl.loop(0, K1S // CHUNK)
    def _(i):
        sums_ref[chunk(i), :] = place(i, blocks, jnp.zeros((CHUNK, HALF), F32))


def place_late_kernel(*refs):
    blocks, early_ref, sums_ref, rounded_ref = refs[:-3], *refs[-3:]

    @pl.loop(0, K1S // CHUNK)
    def _(i):
        total = place(i, blocks, early_ref[chunk(i), :])
        sums_ref[chunk(i), :] = total
        rounded_ref[chunk(i), :] = total.astype(BF16)


def count_kernel(*refs):
    blocks, counts_ref = refs[:-1], refs[-1]

    @pl.loop(0, K1S // CHUNK)
    def _(i):
        count = jnp.zeros((CHUNK, 8), F32)
        for ref in blocks:
            hot, tags = hot_rows(i * CHUNK, CHUNK, ref)
            count += lax.dot_general(hot, tags, NT, preferred_element_type=F32)
        counts_ref[chunk(i), :] = count


TILE = 1024


def finish_kernel(sums_ref, tally_ref, last_ref, mine_ref, squares_ref, counts_ref):
    @pl.loop(0, K1S // CHUNK)
    def _(i):
        at = chunk(i)
        hot, tags = hot_rows(i * CHUNK, CHUNK, last_ref)
        counts_ref[at, :] = tally_ref[at, :] + lax.dot_general(hot, tags, NT, preferred_element_type=F32)
        mine = sums_ref[at, :] + jnp.dot(hot, last_ref[:SLOTS, :], preferred_element_type=F32)
        square = jnp.sum(mine * mine, axis=1, keepdims=True)
        mine_ref[at, :] = mine.astype(BF16)
        squares_ref[at, :] = jnp.broadcast_to(square, (CHUNK, LANES))


def score_kernel(
    mine_ref, squares_ref, counts_ref, partner_ref, last_ref, last_partner_ref, two_ref,
    means_ref, scores_ref, partner, inverse,
):
    w = lax.axis_index("wide")
    core = w % 2

    def score():
        own = pl.ds(pl.multiple_of(core * HALF, HALF), HALF)
        other = pl.ds(pl.multiple_of((1 - core) * HALF, HALF), HALF)
        product = lax.dot_general(mine_ref[...], two_ref[:, own], NT, preferred_element_type=F32)
        product += lax.dot_general(partner[...], two_ref[:, other], NT, preferred_element_type=F32)
        scale = jnp.concatenate([inverse[...]] * (TILE // LANES), axis=1)
        scores_ref[...] = (product * scale).astype(BF16)

    @pl.when(pl.program_id(0) == 0)
    def _():
        hot, _ = hot_rows(0, K1S, last_ref)
        across = partner_ref[...].astype(F32) + jnp.dot(
            hot, last_partner_ref[:SLOTS, :], preferred_element_type=F32
        )
        partner[...] = across.astype(BF16)
        square = squares_ref[...] + jnp.sum(across * across, axis=1, keepdims=True)
        inverse[...] = 1.0 / jnp.sqrt(square + 1e-06)
        lanes = pl.ds(pl.multiple_of(w % 16 // 4 * LANES, LANES), LANES)
        mean = jnp.where(w // 16 == core, mine_ref[:, lanes].astype(F32), partner[:, lanes].astype(F32))
        mean = pltpu.roll(mean, (4 - w % 4) % 4 * 32, 1)
        means_ref[...] = (mean / jnp.maximum(counts_ref[:, 2:3], 1.0)).T[:32]
        score()

    @pl.when(pl.program_id(0) > 0)
    def _():
        score()


def whole(shape):
    return pl.BlockSpec(shape, lambda *_: (0,) * len(shape), pipeline_mode=pl.Buffered(1))


def cost(flops, moved):
    return pl.CostEstimate(flops=flops, bytes_accessed=moved, transcendentals=0)


def local(points, seg_lengths, seg_owner, seg_row, level_two):
    vmem = pl.BlockSpec(memory_space=pltpu.VMEM)
    send = pl.pallas_call(
        pack_kernel,
        out_shape=pltpu.VMEM((SLOTS, HALF + LANES), BF16),
        in_specs=[vmem] * 4,
        out_specs=vmem,
        name="pack",
    )(points, seg_lengths, seg_owner.reshape(1, SEGS), seg_row)
    received = lax.all_to_all(send, ALL, 0, 0, axis_index_groups=PLANES, tiled=True)
    block = pl.pallas_call(
        block_kernel,
        out_shape=pltpu.VMEM((BLOCK, HALF), BF16),
        in_specs=[vmem],
        out_specs=vmem,
        name="block",
    )(received)

    def placer(kernel, flops, out_shape, *operands):
        return pl.pallas_call(
            kernel,
            out_shape=out_shape,
            in_specs=[vmem] * len(operands),
            out_specs=jax.tree.map(lambda _: vmem, out_shape),
            compiler_params=pltpu.CompilerParams(vmem_limit_bytes=16 << 20),
            cost_estimate=cost(flops, 4 << 20),
            name=kernel.__name__[:-7],
        )(*operands)

    up = down = block
    blocks = [block]
    for _ in range(3):
        up, down = lax.ppermute(up, "wide", Z_UP), lax.ppermute(down, "wide", Z_DOWN)
        blocks += [up, down]
    last = lax.ppermute(down, "wide", Z_DOWN)

    totals, halves, tallies, squares_shape = [
        jax.ShapeDtypeStruct((K1S, n), t) for n, t in ((HALF, F32), (HALF, BF16), (8, F32), (LANES, F32))
    ]
    level_two, token = pl.pallas_call(
        fetch_kernel,
        out_shape=(pltpu.VMEM((K2S, D), BF16), jax.ShapeDtypeStruct((8, LANES), F32)),
        in_specs=[pl.BlockSpec(memory_space=pl.ANY)],
        out_specs=(vmem, vmem),
        scratch_shapes=[pltpu.SemaphoreType.DMA],
        compiler_params=pltpu.CompilerParams(vmem_limit_bytes=12 << 20),
        cost_estimate=cost(3 << 30, 8 << 20),
        name="fetch",
    )(level_two)
    early = placer(place_early_kernel, 24 << 30, totals, *blocks[:5], token)
    sums, rounded = placer(place_late_kernel, 24 << 30, (totals, halves), up, down, early)
    partner = lax.ppermute(rounded, "wide", CORE_SWAP)
    tally = placer(count_kernel, 1 << 20, tallies, *blocks)
    last_partner = lax.ppermute(last, "wide", CORE_SWAP)
    mine, squares, counts = placer(
        finish_kernel, 24 << 30, (halves, squares_shape, tallies), sums, tally, last
    )

    means, scores = pl.pallas_call(
        score_kernel,
        grid=(K2S // TILE,),
        out_shape=(
            jax.ShapeDtypeStruct((32, K1S), F32),
            jax.ShapeDtypeStruct((K1S, K2S), BF16),
        ),
        in_specs=[
            *[vmem] * 6,
            pl.BlockSpec((TILE, D), lambda j: (j, 0)),
        ],
        out_specs=(whole((32, K1S)), pl.BlockSpec((K1S, TILE), lambda j: (0, j))),
        scratch_shapes=[pltpu.VMEM((K1S, HALF), BF16), pltpu.VMEM((K1S, LANES), F32)],
        compiler_params=pltpu.CompilerParams(vmem_limit_bytes=32 << 20),
        cost_estimate=cost(14 << 30, 24 << 20),
        name="score",
    )(mine, squares, counts, partner, last, last_partner, level_two)
    return means.T, scores


def solution(mesh):
    return jax.shard_map(
        local,
        mesh=mesh,
        in_specs=(
            P(ALL, None),
            P(ALL, None),
            P(ALL, None, None),
            P(ALL, None),
            P("wide", None),
        ),
        out_specs=(P("narrow", "wide"), P("narrow", "wide")),
        check_vma=False,
    )
```

```python
import jax
import jax.numpy as jnp
from jax import lax
from jax.experimental import pallas as pl
from jax.experimental.pallas import tpu as pltpu
from jax.sharding import PartitionSpec as P

K1S = 1536
K2S = 4096
D = 1024
HALF = 512
SEGS = 32
CAP = 8
NARROW = 8
SLOTS = 256
BLOCK = 264
LANES = 128
F32 = jnp.float32
BF16 = jnp.bfloat16

ALL = ("wide", "narrow")


def wide_of(x, z, c):
    return (x * 8 + z % 8) * 2 + c


WIDES = [(x, z, c) for x in range(2) for z in range(8) for c in range(2)]
PLANES = [
    [wide_of(x, z, c) * NARROW + n for x in range(2) for c in range(2) for n in range(NARROW)]
    for z in range(8)
]
CORE_SWAP = [(wide_of(x, z, c), wide_of(x, z, 1 - c)) for x, z, c in WIDES]
Z_UP = [(wide_of(x, z, c), wide_of(x, z + 1, c)) for x, z, c in WIDES]
Z_DOWN = [(wide_of(x, z, c), wide_of(x, z - 1, c)) for x, z, c in WIDES]


def iota2(shape, axis):
    return lax.broadcasted_iota(jnp.int32, shape, axis)


def pack_kernel(points_ref, lengths_ref, owner_ref, rows_ref, out_ref):
    r, q = iota2((SEGS, SEGS), 0), iota2((SEGS, SEGS), 1)
    eye = (r == q).astype(F32)
    length_row = lengths_ref[...].astype(F32)
    id_row = rows_ref[...].astype(F32)
    owner_row = owner_ref[...].astype(F32)
    length = jnp.sum(eye * length_row, axis=1, keepdims=True)
    ends = jnp.sum(jnp.where(q <= r, length_row, 0.0), axis=1, keepdims=True)
    ids = jnp.sum(eye * id_row, axis=1, keepdims=True)
    owner = jnp.sum(eye * owner_row, axis=1, keepdims=True)
    position = iota2((SEGS, 256), 1).astype(F32)
    member = ((position >= ends - length) & (position < ends)).astype(BF16)
    runs = jnp.dot(member, points_ref[...], preferred_element_type=F32).astype(BF16)

    rank_row = jnp.sum(jnp.where((owner == owner_row) & (r < q), 1.0, 0.0), axis=0, keepdims=True)
    slot_row = owner_row * CAP + rank_row
    place = (iota2((NARROW * CAP, SEGS), 0).astype(F32) == slot_row).astype(BF16)
    slots = jnp.dot(place, runs, preferred_element_type=F32).astype(BF16)
    high = jnp.floor(ids * (1.0 / 16.0))
    low = ids - 16.0 * high
    lane = iota2((SEGS, LANES), 1)
    tags = jnp.where(lane == 0, high, jnp.where(lane == 1, low, jnp.where(lane == 2, length, 0.0)))
    tags = jnp.dot(place, tags.astype(BF16), preferred_element_type=F32).astype(BF16)
    per = NARROW * CAP
    for x in range(2):
        for c in range(2):
            at = pl.ds((x * 2 + c) * per, per)
            out_ref[at, :HALF] = slots[:, c * HALF : (c + 1) * HALF]
            out_ref[at, HALF:] = tags


def block_kernel(received_ref, out_ref):
    out_ref[:SLOTS, :] = received_ref[:, :HALF]
    tags = received_ref[:, HALF:].astype(F32)
    turned = jnp.concatenate([tags[:LANES].T[:8], tags[LANES:].T[:8]], axis=1)
    out_ref[SLOTS:, :SLOTS] = turned.astype(BF16)
    out_ref[SLOTS:, SLOTS:] = jnp.zeros((8, HALF - SLOTS), BF16)


CHUNK = 768
NT = (((1,), (1,)), ((), ()))


def hot_rows(start, rows, ref):
    tags = ref[SLOTS:, :SLOTS]
    ids = tags[0:1].astype(F32) * 16.0 + tags[1:2].astype(F32)
    row = (iota2((rows, SLOTS), 0) + start).astype(F32)
    return (row == ids).astype(BF16), tags


def chunk(i):
    return pl.ds(pl.multiple_of(i * CHUNK, CHUNK), CHUNK)


def place(i, blocks, total):
    for ref in blocks:
        total += jnp.dot(hot_rows(i * CHUNK, CHUNK, ref)[0], ref[:SLOTS, :], preferred_element_type=F32)
    return total


def fetch_kernel(two_ref, out_ref, token_ref, arrived):
    copy = pltpu.make_async_copy(two_ref, out_ref, arrived)
    copy.start()
    token_ref[...] = jnp.zeros_like(token_ref)
    copy.wait()


def place_early_kernel(*refs):
    blocks, sums_ref = refs[:-2], refs[-1]

    @pl.loop(0, K1S // CHUNK)
    def _(i):
        sums_ref[chunk(i), :] = place(i, blocks, jnp.zeros((CHUNK, HALF), F32))


def place_late_kernel(*refs):
    blocks, early_ref, sums_ref, rounded_ref = refs[:-3], *refs[-3:]

    @pl.loop(0, K1S // CHUNK)
    def _(i):
        total = place(i, blocks, early_ref[chunk(i), :])
        sums_ref[chunk(i), :] = total
        rounded_ref[chunk(i), :] = total.astype(BF16)


def count_kernel(*refs):
    blocks, counts_ref = refs[:-1], refs[-1]

    @pl.loop(0, K1S // CHUNK)
    def _(i):
        count = jnp.zeros((CHUNK, 8), F32)
        for ref in blocks:
            hot, tags = hot_rows(i * CHUNK, CHUNK, ref)
            count += lax.dot_general(hot, tags, NT, preferred_element_type=F32)
        counts_ref[chunk(i), :] = count


TILE = 1024


def finish_kernel(sums_ref, tally_ref, last_ref, mine_ref, squares_ref, counts_ref, hot_ref):
    @pl.loop(0, K1S // CHUNK)
    def _(i):
        at = chunk(i)
        hot, tags = hot_rows(i * CHUNK, CHUNK, last_ref)
        hot_ref[at, :] = hot
        count = tally_ref[at, :] + lax.dot_general(hot, tags, NT, preferred_element_type=F32)
        counts_ref[at, :] = jnp.broadcast_to(jnp.maximum(count[:, 2:3], 1.0), (CHUNK, LANES))
        mine = sums_ref[at, :] + jnp.dot(hot, last_ref[:SLOTS, :], preferred_element_type=F32)
        square = jnp.sum(mine * mine, axis=1, keepdims=True)
        mine_ref[at, :] = mine.astype(BF16)
        squares_ref[at, :] = jnp.broadcast_to(square, (CHUNK, LANES))


def score_kernel(
    mine_ref, squares_ref, counts_ref, partner_ref, hot_ref, last_partner_ref, two_ref,
    means_ref, scores_ref, partner, inverse,
):
    w = lax.axis_index("wide")
    core = w % 2

    def score():
        own = pl.ds(pl.multiple_of(core * HALF, HALF), HALF)
        other = pl.ds(pl.multiple_of((1 - core) * HALF, HALF), HALF)
        product = lax.dot_general(mine_ref[...], two_ref[:, own], NT, preferred_element_type=F32)
        product += lax.dot_general(partner[...], two_ref[:, other], NT, preferred_element_type=F32)
        scale = jnp.concatenate([inverse[...]] * (TILE // LANES), axis=1)
        scores_ref[...] = (product * scale).astype(BF16)

    @pl.when(pl.program_id(0) == 0)
    def _():
        across = partner_ref[...].astype(F32) + jnp.dot(
            hot_ref[...], last_partner_ref[:SLOTS, :], preferred_element_type=F32
        )
        partner[...] = across.astype(BF16)
        square = squares_ref[...] + jnp.sum(across * across, axis=1, keepdims=True)
        inverse[...] = 1.0 / jnp.sqrt(square + 1e-06)
        lanes = pl.ds(pl.multiple_of(w % 16 // 4 * LANES, LANES), LANES)
        mean = jnp.where(w // 16 == core, mine_ref[:, lanes].astype(F32), partner[:, lanes].astype(F32))
        mean = pltpu.roll(mean, (4 - w % 4) % 4 * 32, 1)
        means_ref[...] = (mean / counts_ref[...]).T[:32]
        score()

    @pl.when(pl.program_id(0) > 0)
    def _():
        score()


def whole(shape):
    return pl.BlockSpec(shape, lambda *_: (0,) * len(shape), pipeline_mode=pl.Buffered(1))


def cost(flops, moved):
    return pl.CostEstimate(flops=flops, bytes_accessed=moved, transcendentals=0)


def local(points, seg_lengths, seg_owner, seg_row, level_two):
    vmem = pl.BlockSpec(memory_space=pltpu.VMEM)
    send = pl.pallas_call(
        pack_kernel,
        out_shape=pltpu.VMEM((SLOTS, HALF + LANES), BF16),
        in_specs=[vmem] * 4,
        out_specs=vmem,
        name="pack",
    )(points, seg_lengths, seg_owner.reshape(1, SEGS), seg_row)
    received = lax.all_to_all(send, ALL, 0, 0, axis_index_groups=PLANES, tiled=True)
    block = pl.pallas_call(
        block_kernel,
        out_shape=pltpu.VMEM((BLOCK, HALF), BF16),
        in_specs=[vmem],
        out_specs=vmem,
        name="block",
    )(received)

    def placer(kernel, flops, out_shape, *operands):
        return pl.pallas_call(
            kernel,
            out_shape=out_shape,
            in_specs=[vmem] * len(operands),
            out_specs=jax.tree.map(lambda _: vmem, out_shape),
            compiler_params=pltpu.CompilerParams(vmem_limit_bytes=16 << 20),
            cost_estimate=cost(flops, 4 << 20),
            name=kernel.__name__[:-7],
        )(*operands)

    up = down = block
    blocks = [block]
    for _ in range(3):
        up, down = lax.ppermute(up, "wide", Z_UP), lax.ppermute(down, "wide", Z_DOWN)
        blocks += [up, down]
    last = lax.ppermute(down, "wide", Z_DOWN)

    totals, halves, tallies, squares_shape = [
        jax.ShapeDtypeStruct((K1S, n), t) for n, t in ((HALF, F32), (HALF, BF16), (8, F32), (LANES, F32))
    ]
    level_two, token = pl.pallas_call(
        fetch_kernel,
        out_shape=(pltpu.VMEM((K2S, D), BF16), jax.ShapeDtypeStruct((8, LANES), F32)),
        in_specs=[pl.BlockSpec(memory_space=pl.ANY)],
        out_specs=(vmem, vmem),
        scratch_shapes=[pltpu.SemaphoreType.DMA],
        compiler_params=pltpu.CompilerParams(vmem_limit_bytes=12 << 20),
        cost_estimate=cost(3 << 30, 8 << 20),
        name="fetch",
    )(level_two)
    hot_shape = jax.ShapeDtypeStruct((K1S, SLOTS), BF16)
    early = placer(place_early_kernel, 24 << 30, totals, *blocks[:5], token)
    sums, rounded = placer(place_late_kernel, 24 << 30, (totals, halves), up, down, early)
    partner = lax.ppermute(rounded, "wide", CORE_SWAP)
    tally = placer(count_kernel, 1 << 20, tallies, *blocks)
    last_partner = lax.ppermute(last, "wide", CORE_SWAP)
    mine, squares, counts, hot = placer(
        finish_kernel, 24 << 30, (halves, squares_shape, squares_shape, hot_shape), sums, tally, last
    )

    means, scores = pl.pallas_call(
        score_kernel,
        grid=(K2S // TILE,),
        out_shape=(
            jax.ShapeDtypeStruct((32, K1S), F32),
            jax.ShapeDtypeStruct((K1S, K2S), BF16),
        ),
        in_specs=[
            *[vmem] * 6,
            pl.BlockSpec((TILE, D), lambda j: (j, 0)),
        ],
        out_specs=(whole((32, K1S)), pl.BlockSpec((K1S, TILE), lambda j: (0, j))),
        scratch_shapes=[pltpu.VMEM((K1S, HALF), BF16), pltpu.VMEM((K1S, LANES), F32)],
        compiler_params=pltpu.CompilerParams(vmem_limit_bytes=32 << 20),
        cost_estimate=cost(14 << 30, 24 << 20),
        name="score",
    )(mine, squares, counts, partner, hot, last_partner, level_two)
    return means.T, scores


def solution(mesh):
    return jax.shard_map(
        local,
        mesh=mesh,
        in_specs=(
            P(ALL, None),
            P(ALL, None),
            P(ALL, None, None),
            P(ALL, None),
            P("wide", None),
        ),
        out_specs=(P("narrow", "wide"), P("narrow", "wide")),
        check_vma=False,
    )
```
